32 devices in a mesh: row: 8 (over z, core), col: 4 (over y, x).
Axes of the slice: x: 2, y: 2, z: 4, core: 2. Of those that a mesh axis runs over, the one named last changes fastest.
Arguments:
- inv_top: float32 [2, 4096, 4096], P(None, 'row', 'col'), may hold values from -0.0625 to 0.0625
- inv_bottom: float32 [2, 4096, 4096], P(None, 'row', 'col'), may hold values from -0.0625 to 0.0625
- lower_panel: float32 [2, 4096, 4096], P(None, 'row', 'col'), may hold values from -0.0625 to 0.0625
- rhs_top: float32 [2, 4096, 128], P(None, 'col'), may hold values from -6 to 6
- rhs_bottom: float32 [2, 4096, 128], P(None, 'row'), may hold values from -6 to 6
- source_xy: float32 [2, 2, 4096], P(None, None, 'col'), may hold values from -20 to 20
- source_depth: float32 [2, 4096], P(None, 'col'), may hold values from -2 to -0.5
- body_label: int32 [2, 4096], P(None, 'col'), may hold values 0 or 1
- field_xy: float32 [2, 24576], P(None, 'row'), may hold values from -20 to 20
- region_label: int32 [24576], P('row'), may hold values 0 or 1
- lid_table: float32 [2, 2], replicated, may hold values from 0.3 to 3
- wave_number: float32 [1], replicated, may hold values from 0.5 to 1.5
Outputs:
- strengths: float32 [2, 2, 4096, 128], P(None, None, 'col')
- elevation: float32 [24576, 2, 128], P(('row', 'col'))
The draws below stay inside these ranges and needn't reach their ends.
All inputs are finite; a program needn't handle non-finite values. No bound on the sum of `body_label` or of `region_label` on one device may be relied on, other than what follows from the above.
Results may differ from the reference program's by a relative error of at most 0.004.
Values sent between devices are 32-bit elements; how exact they have to be, the bound alone decides.
A program may use at most 64 MiB of HBM per device.

```python
import math
import jax
import jax.numpy as jnp
from jax import lax

B = 4096
R = 128
FIELD_ROW = 3072
SOURCES = 8192
FIELD = 24576
N_ROW = 8


def set_ends(values, stream_key, smallest, top_value):
    place = [jax.random.randint(jax.random.fold_in(stream_key, axis), (), 0, length) for axis, length in enumerate(values.shape)]
    widest = values.shape.index(max(values.shape))
    next_to = place[:widest] + [(place[widest] + 1) % values.shape[widest]] + place[widest + 1:]
    return values.at[tuple(place)].set(smallest).at[tuple(next_to)].set(top_value)


def block_scale(key, dims, cuts, smallest, largest):
    factor_of = 1.0
    for axis_at, blocks in cuts:
        draws = jax.random.uniform(jax.random.fold_in(jax.random.fold_in(key, 6), axis_at), (blocks,), jnp.float32, smallest / len(cuts), largest / len(cuts))
        factor_of = factor_of * jnp.repeat(jnp.exp(draws), dims[axis_at] // blocks).reshape((-1,) + (1,) * (len(dims) - 1 - axis_at))
    return factor_of


def noise(rng, shape, spread, reach, split=(), held_as=jnp.bfloat16):
    factor_of = block_scale(rng, shape, split, -0.22, 0.18) if split else 1.0
    entries = jax.random.normal(rng, shape, jnp.float32) * spread * factor_of
    return jnp.minimum(jnp.maximum(entries, -reach), reach).astype(held_as)


def setup_inputs(seed: int = 0) -> dict:
    arg_keys = jax.random.split(jax.random.key(seed), 13)
    return {
        "inv_top": noise(arg_keys[0], (2, B, B), (2 * B) ** -0.5, 0.0625, ((1, 8), (2, 4)), jnp.float32),
        "inv_bottom": noise(arg_keys[1], (2, B, B), (2 * B) ** -0.5, 0.0625, ((1, 8), (2, 4)), jnp.float32),
        "lower_panel": noise(arg_keys[2], (2, B, B), (2 * B) ** -0.5, 0.0625, ((1, 8), (2, 4)), jnp.float32),
        "rhs_top": noise(arg_keys[3], (2, B, R), 1.0, 6.0, ((1, 4),), jnp.float32),
        "rhs_bottom": noise(arg_keys[4], (2, B, R), 1.0, 6.0, ((1, 8),), jnp.float32),
        "source_xy": jnp.clip(jax.random.uniform(arg_keys[5], (2, 2, B), jnp.float32, -20.0, 20.0) * block_scale(arg_keys[5], (2, 2, B), ((2, 4),), -0.4, 0.0), -20.0, 20.0),
        "source_depth": jnp.clip(-2.0 + 1.5 * jax.random.uniform(arg_keys[6], (2, B), jnp.float32) ** block_scale(arg_keys[6], (2, B), ((1, 4),), -0.2, 0.2), -2.0, -0.5),
        "body_label": set_ends((jax.random.randint(arg_keys[7], (2, B), 0, 2) < 1).astype(jnp.int32), jax.random.fold_in(arg_keys[7], 1), 0, 1),
        "field_xy": jnp.clip(jax.random.uniform(arg_keys[8], (2, FIELD), jnp.float32, -20.0, 20.0) * block_scale(arg_keys[8], (2, FIELD), ((1, 8),), -0.4, 0.0), -20.0, 20.0),
        "region_label": set_ends((jax.random.randint(arg_keys[9], (FIELD,), 0, 2) < 1).astype(jnp.int32), jax.random.fold_in(arg_keys[9], 1), 0, 1),
        "lid_table": jnp.clip(jnp.exp(jax.random.uniform(arg_keys[10], (2, 2), jnp.float32, math.log(0.3), math.log(3.0))), 0.3, 3.0),
        "wave_number": jnp.clip(jnp.exp(jax.random.uniform(arg_keys[11], (1,), jnp.float32, math.log(0.5), math.log(1.5))), 0.5, 1.5),
    }


def complex_product(matrix, vector):
    highest = lax.Precision.HIGHEST
    real_part = jnp.dot(matrix[0], vector[0], precision=highest, preferred_element_type=jnp.float32) - jnp.dot(matrix[1], vector[1], precision=highest, preferred_element_type=jnp.float32)
    imag_part = jnp.dot(matrix[0], vector[1], precision=highest, preferred_element_type=jnp.float32) + jnp.dot(matrix[1], vector[0], precision=highest, preferred_element_type=jnp.float32)
    return jnp.stack([real_part, imag_part])

def green_tile(point_x, point_y, region, source_x, source_y, src_depth, src_label, lid_table, wave_value):
    delta_x = point_x[:, None] - source_x[None, :]
    delta_y = point_y[:, None] - source_y[None, :]
    distance = jnp.sqrt(delta_x * delta_x + delta_y * delta_y + (src_depth * src_depth)[None, :])
    lid_first = jnp.where(region == 1, lid_table[1, 0], lid_table[0, 0])
    lid_second = jnp.where(region == 1, lid_table[1, 1], lid_table[0, 1])
    factor = jnp.where(src_label[None, :] == 1, lid_second[:, None], lid_first[:, None])
    amplitude = factor * jnp.exp(wave_value * src_depth)[None, :] / distance
    phase_angle = wave_value * distance
    return ((amplitude * jnp.cos(phase_angle)).astype(jnp.bfloat16), (amplitude * jnp.sin(phase_angle)).astype(jnp.bfloat16))

def reference(inv_top, inv_bottom, lower_panel, rhs_top, rhs_bottom, source_xy, source_depth, body_label, field_xy, region_label, lid_table, wave_number):
    highest = lax.Precision.HIGHEST
    top_solved = complex_product(inv_top, rhs_top)
    remainder = rhs_bottom - complex_product(lower_panel, top_solved)
    bottom_solved = complex_product(inv_bottom, remainder)
    strengths = jnp.stack([top_solved, bottom_solved])
    weights_low = strengths.astype(jnp.bfloat16)
    weights = lax.optimization_barrier(weights_low).astype(jnp.float32)
    src_real = weights[:, 0].reshape(SOURCES, R)
    src_imag = weights[:, 1].reshape(SOURCES, R)
    source_x = source_xy[0].reshape(-1)
    source_y = source_xy[1].reshape(-1)
    src_depth = source_depth.reshape(-1)
    src_label = body_label.reshape(-1)
    wave_value = wave_number[0]
    blocks_xy = field_xy.reshape(2, N_ROW, FIELD_ROW).transpose(1, 0, 2)
    blocks_region = region_label.reshape(N_ROW, FIELD_ROW)

    def one_block(inputs):
        block_xy, block_region = inputs
        tile_real, tile_imag = green_tile(block_xy[0], block_xy[1], block_region, source_x, source_y, src_depth, src_label, lid_table, wave_value)
        tile_real = lax.optimization_barrier(tile_real).astype(jnp.float32)
        tile_imag = lax.optimization_barrier(tile_imag).astype(jnp.float32)
        real_part = jnp.dot(tile_real, src_real, precision=highest, preferred_element_type=jnp.float32) - jnp.dot(tile_imag, src_imag, precision=highest, preferred_element_type=jnp.float32)
        imag_part = jnp.dot(tile_real, src_imag, precision=highest, preferred_element_type=jnp.float32) + jnp.dot(tile_imag, src_real, precision=highest, preferred_element_type=jnp.float32)
        return jnp.stack([real_part, imag_part], axis=1)
    elevation = lax.map(one_block, (blocks_xy, blocks_region)).reshape(N_ROW * FIELD_ROW, 2, R)
    return (strengths, elevation)
```

```python
import functools
import math

import jax
import jax.numpy as jnp
from jax import lax
from jax.experimental import pallas as pl
from jax.experimental.pallas import tpu as pltpu
from jax.sharding import PartitionSpec as P

SINE = (4.4428679, -7.30744342, 3.59478806, -0.78437397)
COSINE = (1.4142135, -6.97885099, 5.73946117, -1.88356297, 0.31069815)
GROUP = 32
CHUNK = 256


def polynomial(coefficients, value):
    total = coefficients[-1]
    for coefficient in coefficients[-2::-1]:
        total = total * value + coefficient
    return total


def green_kernel(points_ref, sources_ref, real_ref, imag_ref):
    def group(index, carry):
        rows = pl.ds(pl.multiple_of(index * GROUP, GROUP), GROUP)
        point = points_ref[rows, :]
        wide = (GROUP, CHUNK)
        point_x = jnp.broadcast_to(point[:, 0:1], wide)
        point_y = jnp.broadcast_to(point[:, 1:2], wide)
        second = jnp.broadcast_to(point[:, 2:3], wide) > 0.5
        for first in range(0, sources_ref.shape[1], CHUNK):
            lanes = slice(first, first + CHUNK)

            def source(row):
                return jnp.broadcast_to(sources_ref[row : row + 1, lanes], wide)

            delta_x = point_x - source(0)
            delta_y = point_y - source(1)
            square = delta_x * delta_x + delta_y * delta_y + source(2)
            inverse = lax.rsqrt(square)
            turns = square * inverse
            amplitude = jnp.where(second, source(4), source(3)) * inverse
            part = turns - jnp.round(turns)
            part_square = part * part
            half_sine = part * polynomial(SINE, part_square)
            half_cosine = polynomial(COSINE, part_square)
            scaled = amplitude * half_sine
            real_ref[rows, lanes] = (amplitude - scaled * half_sine).astype(jnp.bfloat16)
            imag_ref[rows, lanes] = (scaled * half_cosine).astype(jnp.bfloat16)
        return carry

    lax.fori_loop(0, points_ref.shape[0] // GROUP, group, 0)


def green_tiles(points, sources):
    point_count, source_count = points.shape[0], sources.shape[1]
    tile = max(t for t in range(GROUP, 257, GROUP) if point_count % t == 0)
    shape = jax.ShapeDtypeStruct((point_count, source_count), jnp.bfloat16)
    entries = point_count * source_count
    return pl.pallas_call(
        green_kernel,
        grid=(point_count // tile,),
        in_specs=[
            pl.BlockSpec((tile, points.shape[1]), lambda i: (i, 0)),
            pl.BlockSpec(sources.shape, lambda i: (0, 0)),
        ],
        out_specs=[pl.BlockSpec((tile, source_count), lambda i: (i, 0))] * 2,
        out_shape=[shape, shape],
        cost_estimate=pl.CostEstimate(
            flops=entries * 4000, bytes_accessed=entries * 4, transcendentals=entries
        ),
        compiler_params=pltpu.CompilerParams(vmem_limit_bytes=24 * 2**20),
    )(points, sources)


def turned(vector):
    count = vector.shape[-1] // 2
    return jnp.concatenate([-vector[:, count:], vector[:, :count]], axis=1)


def per_device(
    inv_top,
    inv_bottom,
    lower_panel,
    rhs_top,
    rhs_bottom,
    source_xy,
    source_depth,
    body_label,
    field_xy,
    region_label,
    lid_table,
    wave_number,
):
    col_rows, right_count = rhs_top.shape[1:]
    col_size = lax.axis_size("col")
    col_index = lax.axis_index("col")

    def product(matrix, vector):
        dot = functools.partial(
            jnp.dot, precision=lax.Precision.HIGH, preferred_element_type=jnp.float32
        )
        return dot(matrix[0], vector) + dot(matrix[1], turned(vector))

    def total_piece(partial_sum):
        return lax.psum_scatter(partial_sum, "col", scatter_dimension=0, tiled=True)

    def whole(piece):
        return lax.all_gather(piece, ("row", "col"), axis=0, tiled=True)

    def own_columns(full):
        return lax.dynamic_slice_in_dim(full, col_index * col_rows, col_rows, 0)

    def flat(pair):
        return jnp.concatenate([pair[0], pair[1]], axis=1)

    wave_value = wave_number[0]
    kappa = wave_value * (0.5 / math.pi)
    decay = kappa * jnp.exp(wave_value * source_depth)
    factors = [
        jnp.where(body_label == 1, lid_table[g, 1], lid_table[g, 0]) * decay for g in range(2)
    ]
    zero = jnp.zeros_like(decay)
    depth_turns = kappa * source_depth
    rows = jnp.stack(
        [
            kappa * source_xy[0],
            kappa * source_xy[1],
            depth_turns * depth_turns,
            factors[0],
            factors[1],
            zero,
            zero,
            zero,
        ]
    )
    rows = lax.all_gather(rows, "col", axis=2, tiled=True)
    out_rows = field_xy.shape[1] // col_size
    start = col_index * out_rows
    point_xy = kappa * lax.dynamic_slice_in_dim(field_xy, start, out_rows, 1)
    region = lax.dynamic_slice_in_dim(region_label, start, out_rows, 0).astype(jnp.float32)
    filler = jnp.zeros((5, out_rows), jnp.float32)
    points = jnp.concatenate([point_xy, region[None], filler]).T

    order = rows.shape[2]
    half = order // 2
    tiles = [
        [green_tiles(points, rows[:, b, h * half : (h + 1) * half]) for h in range(2)]
        for b in range(2)
    ]

    def term(block, full):
        weights = full.astype(jnp.bfloat16)
        crossed = turned(weights)
        total = 0.0
        for h in range(2):
            part = slice(h * half, (h + 1) * half)
            real, imag = tiles[block][h]
            total = total + jnp.dot(real, weights[part], preferred_element_type=jnp.float32)
            total = total + jnp.dot(imag, crossed[part], preferred_element_type=jnp.float32)
        return total

    top_full = whole(total_piece(product(inv_top, flat(rhs_top))))
    top_solved = own_columns(top_full)
    panel_piece = total_piece(product(lower_panel, top_solved))
    piece_rows = panel_piece.shape[0]
    rhs_piece = flat(lax.dynamic_slice_in_dim(rhs_bottom, col_index * piece_rows, piece_rows, 1))
    remainder = own_columns(whole(rhs_piece - panel_piece))
    bottom_full = whole(total_piece(product(inv_bottom, remainder)))
    bottom_solved = own_columns(bottom_full)

    elevation = term(0, top_full) + term(1, bottom_full)
    strengths = jnp.stack([top_solved, bottom_solved]).reshape(2, col_rows, 2, right_count)
    return (
        strengths.transpose(0, 2, 1, 3),
        elevation.reshape(out_rows, 2, right_count),
    )


def solution(mesh):
    in_specs = (
        P(None, "row", "col"),
        P(None, "row", "col"),
        P(None, "row", "col"),
        P(None, "col", None),
        P(None, "row", None),
        P(None, None, "col"),
        P(None, "col"),
        P(None, "col"),
        P(None, "row"),
        P("row"),
        P(),
        P(),
    )
    out_specs = (P(None, None, "col", None), P(("row", "col"), None, None))
    return jax.shard_map(
        per_device, mesh=mesh, in_specs=in_specs, out_specs=out_specs, check_vma=False
    )
```

```python
import functools
import math

import jax
import jax.numpy as jnp
from jax import lax
from jax.experimental import pallas as pl
from jax.experimental.pallas import tpu as pltpu
from jax.sharding import PartitionSpec as P

SINE = (4.4428679, -7.30744342, 3.59478806, -0.78437397)
COSINE = (1.4142135, -6.97885099, 5.73946117, -1.88356297, 0.31069815)
GROUP = 32
CHUNK = 256


def polynomial(coefficients, value):
    total = coefficients[-1]
    for coefficient in coefficients[-2::-1]:
        total = total * value + coefficient
    return total


def green_kernel(points_ref, sources_ref, real_ref, imag_ref):
    def group(index, carry):
        rows = pl.ds(pl.multiple_of(index * GROUP, GROUP), GROUP)
        point = points_ref[rows, :]
        wide = (GROUP, CHUNK)
        point_x = jnp.broadcast_to(point[:, 0:1], wide)
        point_y = jnp.broadcast_to(point[:, 1:2], wide)
        second = jnp.broadcast_to(point[:, 2:3], wide) > 0.5
        for first in range(0, sources_ref.shape[1], CHUNK):
            lanes = slice(first, first + CHUNK)

            def source(row):
                return jnp.broadcast_to(sources_ref[row : row + 1, lanes], wide)

            delta_x = point_x - source(0)
            delta_y = point_y - source(1)
            square = delta_x * delta_x + delta_y * delta_y + source(2)
            inverse = lax.rsqrt(square)
            turns = square * inverse
            amplitude = jnp.where(second, source(4), source(3)) * inverse
            part = turns - jnp.round(turns)
            part_square = part * part
            half_sine = part * polynomial(SINE, part_square)
            half_cosine = polynomial(COSINE, part_square)
            scaled = amplitude * half_sine
            real_ref[rows, lanes] = (amplitude - scaled * half_sine).astype(jnp.bfloat16)
            imag_ref[rows, lanes] = (scaled * half_cosine).astype(jnp.bfloat16)
        return carry

    lax.fori_loop(0, points_ref.shape[0] // GROUP, group, 0)


def green_tiles(points, sources):
    point_count, source_count = points.shape[0], sources.shape[1]
    tile = max(t for t in range(GROUP, 257, GROUP) if point_count % t == 0)
    shape = jax.ShapeDtypeStruct((point_count, source_count), jnp.bfloat16)
    entries = point_count * source_count
    return pl.pallas_call(
        green_kernel,
        grid=(point_count // tile,),
        in_specs=[
            pl.BlockSpec((tile, points.shape[1]), lambda i: (i, 0)),
            pl.BlockSpec(sources.shape, lambda i: (0, 0)),
        ],
        out_specs=[pl.BlockSpec((tile, source_count), lambda i: (i, 0))] * 2,
        out_shape=[shape, shape],
        cost_estimate=pl.CostEstimate(
            flops=entries * 4000, bytes_accessed=entries * 4, transcendentals=entries
        ),
        compiler_params=pltpu.CompilerParams(vmem_limit_bytes=24 * 2**20),
    )(points, sources)


def round_kernel(full_ref, weights_ref, crossed_ref):
    count = full_ref.shape[1] // 2
    real = full_ref[:, :count]
    imag = full_ref[:, count:]
    weights_ref[:, :count] = real.astype(jnp.bfloat16)
    weights_ref[:, count:] = imag.astype(jnp.bfloat16)
    crossed_ref[:, :count] = (-imag).astype(jnp.bfloat16)
    crossed_ref[:, count:] = real.astype(jnp.bfloat16)


def rounded(full):
    tile = full.shape[0] // 4
    shape = jax.ShapeDtypeStruct(full.shape, jnp.bfloat16)
    spec = pl.BlockSpec((tile, full.shape[1]), lambda i: (i, 0))
    return pl.pallas_call(
        round_kernel,
        grid=(4,),
        in_specs=[spec],
        out_specs=[spec, spec],
        out_shape=[shape, shape],
        compiler_params=pltpu.CompilerParams(vmem_limit_bytes=24 * 2**20),
    )(full)


def turned(vector):
    count = vector.shape[-1] // 2
    return jnp.concatenate([-vector[:, count:], vector[:, :count]], axis=1)


def per_device(
    inv_top,
    inv_bottom,
    lower_panel,
    rhs_top,
    rhs_bottom,
    source_xy,
    source_depth,
    body_label,
    field_xy,
    region_label,
    lid_table,
    wave_number,
):
    col_rows, right_count = rhs_top.shape[1:]
    col_size = lax.axis_size("col")
    col_index = lax.axis_index("col")

    def product(matrix, vector):
        dot = functools.partial(
            jnp.dot, precision=lax.Precision.HIGH, preferred_element_type=jnp.float32
        )
        return dot(matrix[0], vector) + dot(matrix[1], turned(vector))

    row_size = lax.axis_size("row")
    row_index = lax.axis_index("row")
    chips = row_size // 2
    per_col = row_size // col_size
    core = row_index % 2

    def shift_col(piece, step):
        pairs = [((i + step) % col_size, i) for i in range(col_size)]
        return lax.ppermute(piece, "col", pairs)

    def shift_chip(piece, step):
        pairs = [((i + 2 * step) % row_size, i) for i in range(row_size)]
        return lax.ppermute(piece, "row", pairs)

    def sibling(piece):
        return lax.ppermute(piece, "row", [(i, i ^ 1) for i in range(row_size)])

    def by_core(mine, other, axis):
        first = jnp.where(core == 0, mine, other)
        second = jnp.where(core == 0, other, mine)
        return jnp.stack([first, second], axis=axis)

    def total_piece(partial_sum):
        piece_rows = partial_sum.shape[0] // col_size

        def piece_of(step):
            place = (col_index - step + col_size) % col_size * piece_rows
            return lax.dynamic_slice_in_dim(partial_sum, place, piece_rows, 0)

        total = piece_of(0)
        for step in range(1, col_size):
            total = total + shift_col(piece_of(step), step)
        return total

    def columns(piece):
        pairs = []
        for r in range(row_size):
            for c in range(col_size):
                target = (r % per_col) * col_size + c
                pairs.append((r * col_size + c, target * col_size + r // per_col))
        piece = lax.ppermute(piece, ("row", "col"), pairs)
        turned_list = [piece] + [shift_chip(piece, step) for step in range(1, chips)]
        ring = jnp.stack(turned_list + turned_list)
        chip = row_index // 2
        mine = lax.dynamic_slice_in_dim(ring, (chips - chip) % chips, chips, 0)
        return by_core(mine, sibling(mine), 1).reshape(-1, piece.shape[1])

    def whole(own):
        half_rows = own.shape[0] // 2
        half = lax.dynamic_slice_in_dim(own, core * half_rows, half_rows, 0)
        mine = [shift_col(half, step) for step in range(1, col_size)]
        mine = jnp.stack(lax.optimization_barrier(mine))
        mine, other = lax.optimization_barrier((mine, sibling(mine)))
        rest = by_core(mine, other, 1).reshape(-1, own.shape[1])
        return jnp.concatenate([own, rest])

    def flat(pair):
        return jnp.concatenate([pair[0], pair[1]], axis=1)

    wave_value = wave_number[0]
    kappa = wave_value * (0.5 / math.pi)
    decay = kappa * jnp.exp(wave_value * source_depth)
    factors = [
        jnp.where(body_label == 1, lid_table[g, 1], lid_table[g, 0]) * decay for g in range(2)
    ]
    zero = jnp.zeros_like(decay)
    depth_turns = kappa * source_depth
    rows = jnp.stack(
        [
            kappa * source_xy[0],
            kappa * source_xy[1],
            depth_turns * depth_turns,
            factors[0],
            factors[1],
            zero,
            zero,
            zero,
        ]
    )
    rows = jnp.concatenate(
        [rows] + [shift_col(rows, step) for step in range(1, col_size)], axis=2
    )
    out_rows = field_xy.shape[1] // col_size
    start = col_index * out_rows
    point_xy = kappa * lax.dynamic_slice_in_dim(field_xy, start, out_rows, 1)
    region = lax.dynamic_slice_in_dim(region_label, start, out_rows, 0).astype(jnp.float32)
    filler = jnp.zeros((5, out_rows), jnp.float32)
    points = jnp.concatenate([point_xy, region[None], filler]).T

    order = rows.shape[2]
    half = order // 2
    tiles = [
        [green_tiles(points, rows[:, b, h * half : (h + 1) * half]) for h in range(2)]
        for b in range(2)
    ]

    def term(block, full):
        weights, crossed = rounded(full)
        total = 0.0
        for h in range(2):
            part = slice(h * half, (h + 1) * half)
            real, imag = tiles[block][h]
            total = total + jnp.dot(real, weights[part], preferred_element_type=jnp.float32)
            total = total + jnp.dot(imag, crossed[part], preferred_element_type=jnp.float32)
        return total

    top_solved = columns(total_piece(product(inv_top, flat(rhs_top))))
    top_full = whole(top_solved)
    panel_piece = total_piece(product(lower_panel, top_solved))
    piece_rows = panel_piece.shape[0]
    rhs_piece = flat(lax.dynamic_slice_in_dim(rhs_bottom, col_index * piece_rows, piece_rows, 1))
    remainder = columns(rhs_piece - panel_piece)
    bottom_solved = columns(total_piece(product(inv_bottom, remainder)))
    bottom_full = whole(bottom_solved)

    elevation = term(0, top_full) + term(1, bottom_full)
    strengths = jnp.stack([top_solved, bottom_solved]).reshape(2, col_rows, 2, right_count)
    return (
        strengths.transpose(0, 2, 1, 3),
        elevation.reshape(out_rows, 2, right_count),
    )


def solution(mesh):
    in_specs = (
        P(None, "row", "col"),
        P(None, "row", "col"),
        P(None, "row", "col"),
        P(None, "col", None),
        P(None, "row", None),
        P(None, None, "col"),
        P(None, "col"),
        P(None, "col"),
        P(None, "row"),
        P("row"),
        P(),
        P(),
    )
    out_specs = (P(None, None, "col", None), P(("row", "col"), None, None))
    return jax.shard_map(
        per_device, mesh=mesh, in_specs=in_specs, out_specs=out_specs, check_vma=False
    )
```

```python
import functools
import math

import jax
import jax.numpy as jnp
from jax import lax
from jax.experimental import pallas as pl
from jax.experimental.pallas import tpu as pltpu
from jax.sharding import PartitionSpec as P

SINE = (4.4428679, -7.30744342, 3.59478806, -0.78437397)
COSINE = (1.4142135, -6.97885099, 5.73946117, -1.88356297, 0.31069815)
GROUP = 32
CHUNK = 256


def polynomial(coefficients, value):
    total = coefficients[-1]
    for coefficient in coefficients[-2::-1]:
        total = total * value + coefficient
    return total


def green_kernel(points_ref, sources_ref, real_ref, imag_ref):
    def group(index, carry):
        rows = pl.ds(pl.multiple_of(index * GROUP, GROUP), GROUP)
        point = points_ref[rows, :]
        wide = (GROUP, CHUNK)
        point_x = jnp.broadcast_to(point[:, 0:1], wide)
        point_y = jnp.broadcast_to(point[:, 1:2], wide)
        second = jnp.broadcast_to(point[:, 2:3], wide) > 0.5
        for first in range(0, sources_ref.shape[1], CHUNK):
            lanes = slice(first, first + CHUNK)

            def source(row):
                return jnp.broadcast_to(sources_ref[row : row + 1, lanes], wide)

            delta_x = point_x - source(0)
            delta_y = point_y - source(1)
            square = delta_x * delta_x + delta_y * delta_y + source(2)
            inverse = lax.rsqrt(square)
            turns = square * inverse
            amplitude = jnp.where(second, source(4), source(3)) * inverse
            part = turns - jnp.round(turns)
            part_square = part * part
            half_sine = part * polynomial(SINE, part_square)
            half_cosine = polynomial(COSINE, part_square)
            scaled = amplitude * half_sine
            real_ref[rows, lanes] = (amplitude - scaled * half_sine).astype(jnp.bfloat16)
            imag_ref[rows, lanes] = (scaled * half_cosine).astype(jnp.bfloat16)
        return carry

    lax.fori_loop(0, points_ref.shape[0] // GROUP, group, 0)


def green_tiles(points, sources):
    point_count, source_count = points.shape[0], sources.shape[1]
    tile = max(t for t in range(GROUP, 257, GROUP) if point_count % t == 0)
    shape = jax.ShapeDtypeStruct((point_count, source_count), jnp.bfloat16)
    entries = point_count * source_count
    return pl.pallas_call(
        green_kernel,
        grid=(point_count // tile,),
        in_specs=[
            pl.BlockSpec((tile, points.shape[1]), lambda i: (i, 0)),
            pl.BlockSpec(sources.shape, lambda i: (0, 0)),
        ],
        out_specs=[pl.BlockSpec((tile, source_count), lambda i: (i, 0))] * 2,
        out_shape=[shape, shape],
        cost_estimate=pl.CostEstimate(
            flops=entries * 4000, bytes_accessed=entries * 4, transcendentals=entries
        ),
        compiler_params=pltpu.CompilerParams(vmem_limit_bytes=24 * 2**20),
    )(points, sources)


def round_kernel(full_ref, weights_ref, crossed_ref):
    count = full_ref.shape[1] // 2
    real = full_ref[:, :count]
    imag = full_ref[:, count:]
    weights_ref[:, :count] = real.astype(jnp.bfloat16)
    weights_ref[:, count:] = imag.astype(jnp.bfloat16)
    crossed_ref[:, :count] = (-imag).astype(jnp.bfloat16)
    crossed_ref[:, count:] = real.astype(jnp.bfloat16)


def rounded(full):
    tile = full.shape[0] // 4
    shape = jax.ShapeDtypeStruct(full.shape, jnp.bfloat16)
    spec = pl.BlockSpec((tile, full.shape[1]), lambda i: (i, 0))
    return pl.pallas_call(
        round_kernel,
        grid=(4,),
        in_specs=[spec],
        out_specs=[spec, spec],
        out_shape=[shape, shape],
        compiler_params=pltpu.CompilerParams(vmem_limit_bytes=24 * 2**20),
    )(full)


def turned(vector):
    count = vector.shape[-1] // 2
    return jnp.concatenate([-vector[:, count:], vector[:, :count]], axis=1)


def per_device(
    inv_top,
    inv_bottom,
    lower_panel,
    rhs_top,
    rhs_bottom,
    source_xy,
    source_depth,
    body_label,
    field_xy,
    region_label,
    lid_table,
    wave_number,
):
    col_rows, right_count = rhs_top.shape[1:]
    col_size = lax.axis_size("col")
    col_index = lax.axis_index("col")

    def product(matrix, vector):
        dot = functools.partial(
            jnp.dot, precision=lax.Precision.HIGH, preferred_element_type=jnp.float32
        )
        return dot(matrix[0], vector) + dot(matrix[1], turned(vector))

    row_size = lax.axis_size("row")
    row_index = lax.axis_index("row")
    chips = row_size // 2
    per_col = row_size // col_size
    core = row_index % 2

    def shift_col(piece, step):
        pairs = [((i + step) % col_size, i) for i in range(col_size)]
        return lax.ppermute(piece, "col", pairs)

    def shift_chip(piece, step):
        pairs = [((i + 2 * step) % row_size, i) for i in range(row_size)]
        return lax.ppermute(piece, "row", pairs)

    def sibling(piece):
        return lax.ppermute(piece, "row", [(i, i ^ 1) for i in range(row_size)])

    def by_core(mine, other, axis):
        first = jnp.where(core == 0, mine, other)
        second = jnp.where(core == 0, other, mine)
        return jnp.stack([first, second], axis=axis)

    def columns(partial_sum, block, half_index):
        piece_rows = partial_sum.shape[0] // col_size
        total = 0.0
        for step in range(col_size):
            pairs = []
            for r in range(row_size):
                for c in range(col_size):
                    target = (r % per_col) * col_size + (c + step) % col_size
                    pairs.append((r * col_size + c, target * col_size + r // per_col))
            place = (col_index + step) % col_size * piece_rows
            piece = lax.dynamic_slice_in_dim(partial_sum, place, piece_rows, 0)
            total = total + lax.ppermute(piece, ("row", "col"), pairs)
        total, source_part = lax.optimization_barrier((total, sources_of(block, half_index)))
        others = [shift_chip(total, step) for step in range(1, chips)]
        others, tile = lax.optimization_barrier((others, green_tiles(points, source_part)))
        tiles[block][half_index] = tile
        turned_list = [total] + others
        ring = jnp.stack(turned_list + turned_list)
        chip = row_index // 2
        mine = lax.dynamic_slice_in_dim(ring, (chips - chip) % chips, chips, 0)
        return by_core(mine, sibling(mine), 1).reshape(-1, total.shape[1])

    def whole(own):
        half_rows = own.shape[0] // 2
        half = lax.dynamic_slice_in_dim(own, core * half_rows, half_rows, 0)
        mine = [shift_col(half, step) for step in range(1, col_size)]
        mine = jnp.stack(lax.optimization_barrier(mine))
        mine, other = lax.optimization_barrier((mine, sibling(mine)))
        rest = by_core(mine, other, 1).reshape(-1, own.shape[1])
        return jnp.concatenate([own, rest])

    def flat(pair):
        return jnp.concatenate([pair[0], pair[1]], axis=1)

    wave_value = wave_number[0]
    kappa = wave_value * (0.5 / math.pi)
    decay = kappa * jnp.exp(wave_value * source_depth)
    factors = [
        jnp.where(body_label == 1, lid_table[g, 1], lid_table[g, 0]) * decay for g in range(2)
    ]
    zero = jnp.zeros_like(decay)
    depth_turns = kappa * source_depth
    rows = jnp.stack(
        [
            kappa * source_xy[0],
            kappa * source_xy[1],
            depth_turns * depth_turns,
            factors[0],
            factors[1],
            zero,
            zero,
            zero,
        ]
    )
    rows = jnp.concatenate(
        [rows] + [shift_col(rows, step) for step in range(1, col_size)], axis=2
    )
    out_rows = field_xy.shape[1] // col_size
    start = col_index * out_rows
    point_xy = kappa * lax.dynamic_slice_in_dim(field_xy, start, out_rows, 1)
    region = lax.dynamic_slice_in_dim(region_label, start, out_rows, 0).astype(jnp.float32)
    filler = jnp.zeros((5, out_rows), jnp.float32)
    points = jnp.concatenate([point_xy, region[None], filler]).T

    order = rows.shape[2]
    half = order // 2
    tiles = [[None, None], [None, None]]

    def sources_of(block, half_index):
        return rows[:, block, half_index * half : (half_index + 1) * half]

    def term(block, full):
        weights, crossed = rounded(full)
        total = 0.0
        for h in range(2):
            part = slice(h * half, (h + 1) * half)
            real, imag = tiles[block][h]
            total = total + jnp.dot(real, weights[part], preferred_element_type=jnp.float32)
            total = total + jnp.dot(imag, crossed[part], preferred_element_type=jnp.float32)
        return total

    top_solved = columns(product(inv_top, flat(rhs_top)), 0, 0)
    top_full = whole(top_solved)
    first_col = (col_index == 0).astype(jnp.float32)
    panel_sum = first_col * flat(rhs_bottom) - product(lower_panel, top_solved)
    remainder = columns(panel_sum, 0, 1)
    bottom_solved = columns(product(inv_bottom, remainder), 1, 0)
    bottom_solved, source_part = lax.optimization_barrier((bottom_solved, sources_of(1, 1)))
    tiles[1][1] = green_tiles(points, source_part)
    bottom_full = whole(bottom_solved)
    top_solved, bottom_solved, bottom_full, tiles[1][1] = lax.optimization_barrier(
        (top_solved, bottom_solved, bottom_full, tiles[1][1])
    )

    elevation = term(0, top_full) + term(1, bottom_full)
    strengths = jnp.stack([top_solved, bottom_solved]).reshape(2, col_rows, 2, right_count)
    return (
        strengths.transpose(0, 2, 1, 3),
        elevation.reshape(out_rows, 2, right_count),
    )


def solution(mesh):
    in_specs = (
        P(None, "row", "col"),
        P(None, "row", "col"),
        P(None, "row", "col"),
        P(None, "col", None),
        P(None, "row", None),
        P(None, None, "col"),
        P(None, "col"),
        P(None, "col"),
        P(None, "row"),
        P("row"),
        P(),
        P(),
    )
    out_specs = (P(None, None, "col", None), P(("row", "col"), None, None))
    return jax.shard_map(
        per_device, mesh=mesh, in_specs=in_specs, out_specs=out_specs, check_vma=False
    )
```

```python
import functools
import math

import jax
import jax.numpy as jnp
from jax import lax
from jax.experimental import pallas as pl
from jax.experimental.pallas import tpu as pltpu
from jax.sharding import PartitionSpec as P

SINE = (4.4428679, -7.30744342, 3.59478806, -0.78437397)
COSINE = (1.4142135, -6.97885099, 5.73946117, -1.88356297, 0.31069815)
GROUP = 32
CHUNK = 256


def polynomial(coefficients, value):
    total = coefficients[-1]
    for coefficient in coefficients[-2::-1]:
        total = total * value + coefficient
    return total


def green_kernel(points_ref, sources_ref, real_ref, imag_ref):
    def group(index, carry):
        rows = pl.ds(pl.multiple_of(index * GROUP, GROUP), GROUP)
        point = points_ref[rows, :]
        wide = (GROUP, CHUNK)
        point_x = jnp.broadcast_to(point[:, 0:1], wide)
        point_y = jnp.broadcast_to(point[:, 1:2], wide)
        second = jnp.broadcast_to(point[:, 2:3], wide) > 0.5
        for first in range(0, sources_ref.shape[1], CHUNK):
            lanes = slice(first, first + CHUNK)

            def source(row):
                return jnp.broadcast_to(sources_ref[row : row + 1, lanes], wide)

            delta_x = point_x - source(0)
            delta_y = point_y - source(1)
            square = delta_x * delta_x + delta_y * delta_y + source(2)
            inverse = lax.rsqrt(square)
            turns = square * inverse
            amplitude = jnp.where(second, source(4), source(3)) * inverse
            part = turns - jnp.round(turns)
            part_square = part * part
            half_sine = part * polynomial(SINE, part_square)
            half_cosine = polynomial(COSINE, part_square)
            scaled = amplitude * half_sine
            real_ref[rows, lanes] = (amplitude - scaled * half_sine).astype(jnp.bfloat16)
            imag_ref[rows, lanes] = (scaled * half_cosine).astype(jnp.bfloat16)
        return carry

    lax.fori_loop(0, points_ref.shape[0] // GROUP, group, 0)


def green_tiles(points, sources):
    point_count, source_count = points.shape[0], sources.shape[1]
    tile = max(t for t in range(GROUP, 257, GROUP) if point_count % t == 0)
    shape = jax.ShapeDtypeStruct((point_count, source_count), jnp.bfloat16)
    entries = point_count * source_count
    return pl.pallas_call(
        green_kernel,
        grid=(point_count // tile,),
        in_specs=[
            pl.BlockSpec((tile, points.shape[1]), lambda i: (i, 0)),
            pl.BlockSpec(sources.shape, lambda i: (0, 0)),
        ],
        out_specs=[pl.BlockSpec((tile, source_count), lambda i: (i, 0))] * 2,
        out_shape=[shape, shape],
        cost_estimate=pl.CostEstimate(
            flops=entries * 4000, bytes_accessed=entries * 4, transcendentals=entries
        ),
        compiler_params=pltpu.CompilerParams(vmem_limit_bytes=24 * 2**20),
    )(points, sources)


def round_kernel(full_ref, weights_ref, crossed_ref):
    count = full_ref.shape[1] // 2
    real = full_ref[:, :count]
    imag = full_ref[:, count:]
    weights_ref[:, :count] = real.astype(jnp.bfloat16)
    weights_ref[:, count:] = imag.astype(jnp.bfloat16)
    crossed_ref[:, :count] = (-imag).astype(jnp.bfloat16)
    crossed_ref[:, count:] = real.astype(jnp.bfloat16)


def rounded(full):
    tile = full.shape[0] // 4
    shape = jax.ShapeDtypeStruct(full.shape, jnp.bfloat16)
    spec = pl.BlockSpec((tile, full.shape[1]), lambda i: (i, 0))
    return pl.pallas_call(
        round_kernel,
        grid=(4,),
        in_specs=[spec],
        out_specs=[spec, spec],
        out_shape=[shape, shape],
        compiler_params=pltpu.CompilerParams(vmem_limit_bytes=24 * 2**20),
    )(full)


def turned(vector):
    count = vector.shape[-1] // 2
    return jnp.concatenate([-vector[:, count:], vector[:, :count]], axis=1)


def per_device(
    inv_top,
    inv_bottom,
    lower_panel,
    rhs_top,
    rhs_bottom,
    source_xy,
    source_depth,
    body_label,
    field_xy,
    region_label,
    lid_table,
    wave_number,
):
    col_rows, right_count = rhs_top.shape[1:]
    col_size = lax.axis_size("col")
    col_index = lax.axis_index("col")

    def product(matrix, vector):
        dot = functools.partial(
            jnp.dot, precision=lax.Precision.HIGH, preferred_element_type=jnp.float32
        )
        return dot(matrix[0], vector) + dot(matrix[1], turned(vector))

    row_size = lax.axis_size("row")
    row_index = lax.axis_index("row")
    chips = row_size // 2
    per_col = row_size // col_size
    core = row_index % 2

    def shift_col(piece, step):
        pairs = [((i + step) % col_size, i) for i in range(col_size)]
        return lax.ppermute(piece, "col", pairs)

    def shift_chip(piece, step):
        pairs = [((i + 2 * step) % row_size, i) for i in range(row_size)]
        return lax.ppermute(piece, "row", pairs)

    def sibling(piece):
        return lax.ppermute(piece, "row", [(i, i ^ 1) for i in range(row_size)])

    def by_core(mine, other, axis):
        first = jnp.where(core == 0, mine, other)
        second = jnp.where(core == 0, other, mine)
        return jnp.stack([first, second], axis=axis)

    def columns(partial_sum, block, half_index):
        piece_rows = partial_sum.shape[0] // col_size
        total = 0.0
        for step in range(col_size):
            pairs = []
            for r in range(row_size):
                for c in range(col_size):
                    target = (r % per_col) * col_size + (c + step) % col_size
                    pairs.append((r * col_size + c, target * col_size + r // per_col))
            place = (col_index + step) % col_size * piece_rows
            piece = lax.dynamic_slice_in_dim(partial_sum, place, piece_rows, 0)
            total = total + lax.ppermute(piece, ("row", "col"), pairs)
        total, source_part = lax.optimization_barrier((total, sources_of(block, half_index)))
        others = [shift_chip(total, step) for step in range(1, chips)]
        others, tile = lax.optimization_barrier((others, green_tiles(points, source_part)))
        tiles[block][half_index] = tile
        turned_list = [total] + others
        ring = jnp.stack(turned_list + turned_list)
        chip = row_index // 2
        mine = lax.dynamic_slice_in_dim(ring, (chips - chip) % chips, chips, 0)
        return by_core(mine, sibling(mine), 1).reshape(-1, total.shape[1])

    def whole(own):
        half_rows = own.shape[0] // 2
        half = lax.dynamic_slice_in_dim(own, core * half_rows, half_rows, 0)
        mine = [shift_col(half, step) for step in range(1, col_size)]
        mine = jnp.stack(lax.optimization_barrier(mine))
        mine, other = lax.optimization_barrier((mine, sibling(mine)))
        rest = by_core(mine, other, 1).reshape(-1, own.shape[1])
        return jnp.concatenate([own, rest])

    def flat(pair):
        return jnp.concatenate([pair[0], pair[1]], axis=1)

    wave_value = wave_number[0]
    kappa = wave_value * (0.5 / math.pi)
    decay = kappa * jnp.exp(wave_value * source_depth)
    factors = [
        jnp.where(body_label == 1, lid_table[g, 1], lid_table[g, 0]) * decay for g in range(2)
    ]
    zero = jnp.zeros_like(decay)
    depth_turns = kappa * source_depth
    rows = jnp.stack(
        [
            kappa * source_xy[0],
            kappa * source_xy[1],
            depth_turns * depth_turns,
            factors[0],
            factors[1],
            zero,
            zero,
            zero,
        ]
    )
    rows = jnp.concatenate(
        [rows] + [shift_col(rows, step) for step in range(1, col_size)], axis=2
    )
    out_rows = field_xy.shape[1] // col_size
    start = col_index * out_rows
    point_xy = kappa * lax.dynamic_slice_in_dim(field_xy, start, out_rows, 1)
    region = lax.dynamic_slice_in_dim(region_label, start, out_rows, 0).astype(jnp.float32)
    filler = jnp.zeros((5, out_rows), jnp.float32)
    points = jnp.concatenate([point_xy, region[None], filler]).T

    order = rows.shape[2]
    half = order // 2
    tiles = [[None, None], [None, None]]

    def sources_of(block, half_index):
        return rows[:, block, half_index * half : (half_index + 1) * half]

    def term(block, full):
        weights, crossed = rounded(full)
        total = 0.0
        for h in range(2):
            part = slice(h * half, (h + 1) * half)
            real, imag = tiles[block][h]
            total = total + jnp.dot(real, weights[part], preferred_element_type=jnp.float32)
            total = total + jnp.dot(imag, crossed[part], preferred_element_type=jnp.float32)
        return total

    top_solved = columns(product(inv_top, flat(rhs_top)), 0, 0)
    top_full = whole(top_solved)
    first_col = (col_index == 0).astype(jnp.float32)
    panel_sum = first_col * flat(rhs_bottom) - product(lower_panel, top_solved)
    remainder = columns(panel_sum, 0, 1)
    bottom_solved = columns(product(inv_bottom, remainder), 1, 0)
    bottom_solved, source_part = lax.optimization_barrier((bottom_solved, sources_of(1, 1)))
    tiles[1][1] = green_tiles(points, source_part)
    bottom_full = whole(bottom_solved)
    top_solved, bottom_solved, tiles[1][1] = lax.optimization_barrier(
        (top_solved, bottom_solved, tiles[1][1])
    )

    elevation = term(0, top_full) + term(1, bottom_full)
    strengths = jnp.stack([top_solved, bottom_solved]).reshape(2, col_rows, 2, right_count)
    return (
        strengths.transpose(0, 2, 1, 3),
        elevation.reshape(out_rows, 2, right_count),
    )


def solution(mesh):
    in_specs = (
        P(None, "row", "col"),
        P(None, "row", "col"),
        P(None, "row", "col"),
        P(None, "col", None),
        P(None, "row", None),
        P(None, None, "col"),
        P(None, "col"),
        P(None, "col"),
        P(None, "row"),
        P("row"),
        P(),
        P(),
    )
    out_specs = (P(None, None, "col", None), P(("row", "col"), None, None))
    return jax.shard_map(
        per_device, mesh=mesh, in_specs=in_specs, out_specs=out_specs, check_vma=False
    )
```
